256 devices in a mesh: dp: 64 (over y_lo, z, x), tensor: 4 (over y_hi, core).
Axes of the slice: x: 4, y: 4 (y_hi: 2, y_lo: 2; y = y_hi * 2 + y_lo), z: 8, core: 2. Of those that a mesh axis runs over, the one named last changes fastest.
Arguments:
- gradient: bfloat16 [16384, 8192], P('tensor', 'dp'), may hold values from -6 to 6
- first_moment: float32 [16384, 8192], P('tensor', 'dp'), may hold values from -6 to 6
- second_moment: float32 [16384, 8192], P('tensor', 'dp'), may hold values from 0.05 to 2
- left_candidates: bfloat16 [64, 4, 1024, 1024], P('dp', 'tensor'), may hold values from -0.1875 to 0.1875
- right_candidates: bfloat16 [64, 4, 512, 512], P('dp', 'tensor'), may hold values from -0.25 to 0.25
- left_owner: int32 [8], replicated, may hold values from 0 to 31
- right_owner: int32 [4, 8], P('tensor'), may hold values from 0 to 63, as said below
Outputs:
- moment_new: float32 [16384, 8192], P('tensor', 'dp')
- second_new: float32 [16384, 8192], P('tensor', 'dp')
- update: bfloat16 [16384, 8192], P('tensor', 'dp')
The draws below stay inside these ranges and needn't reach their ends.
Inputs may be any that keep to these rules, and one draw needn't show every extreme that they name: `right_owner`: each row holds 8 distinct dp indices; 0 and 64 - 1 are among them.
All inputs are finite; a program needn't handle non-finite values.
Results may differ from the reference program's by a relative error of at most 0.007.
Values may be sent and summed in bfloat16 or wider, within the bound.
A program may use at most 128 MiB of HBM per device.

```python
import math
import jax
import jax.numpy as jnp

D = 8192
LB = 1024
RB = 512
CB_DEV = 8
NRB = 8
COLS = 16384
GROUP = 8
N_DP = 64
N_TENSOR = 4


def pick_owners(key, count):
    first_key = jax.random.fold_in(key, 11)
    second_key = jax.random.fold_in(key, 12)
    middle = jax.random.permutation(first_key, N_DP - 2)[:count - 2].astype(jnp.int32) + 1
    chosen = jnp.concatenate([jnp.array([0, N_DP - 1], dtype=jnp.int32), middle])
    return jax.random.permutation(second_key, chosen).astype(jnp.int32)


def draw_right_owner(key, part):
    key = jax.random.fold_in(key, 2)
    return jnp.stack([pick_owners(jax.random.fold_in(key, 100 + tensor_row), CB_DEV) for tensor_row in range(N_TENSOR)])


def with_ends(values, key, smallest, top_value):
    longest = values.shape.index(max(values.shape))
    spots = []
    for shift in (0, 1):
        where = [jax.random.randint(jax.random.fold_in(key, axis), (), 0, length) for axis, length in enumerate(values.shape)]
        where[longest] = (where[longest] + shift) % values.shape[longest]
        spots.append(tuple(where))
    return values.at[spots[0]].set(smallest).at[spots[1]].set(top_value)


def shard_levels(stream_key, extent, shards, smallest, largest):
    def one(axis_at, blocks):
        draws = jax.random.uniform(jax.random.fold_in(jax.random.fold_in(stream_key, 6), axis_at), (blocks,), jnp.float32, smallest / len(shards), largest / len(shards))
        return jnp.repeat(jnp.exp(draws), extent[axis_at] // blocks).reshape((-1,) + (1,) * (len(extent) - axis_at - 1))

    loudness = one(*shards[0])
    for cut in shards[1:]:
        loudness = loudness * one(*cut)
    return loudness


def normal_values(rng, shape, width, limit, split=(), kind=jnp.bfloat16):
    gain = shard_levels(rng, shape, split, -0.22, 0.18) if split else 1.0
    values = jax.random.normal(rng, shape, jnp.float32) * width * gain
    return jnp.minimum(jnp.maximum(values, -limit), limit).astype(kind)


def setup_inputs(seed: int = 0) -> dict:
    streams_of = jax.random.split(jax.random.key(seed), 8)
    gradient = normal_values(streams_of[0], (COLS, D), 1.0, 6.0, ((0, 4), (1, 64)))
    first_moment = normal_values(streams_of[1], (COLS, D), 1.0, 6.0, ((0, 4), (1, 64)), jnp.float32)
    second_moment = jnp.clip(jnp.exp(math.log(2.0) - 3.6888794 * jax.random.uniform(streams_of[2], (COLS, D), jnp.float32) ** shard_levels(streams_of[2], (COLS, D), ((0, 4), (1, 64)), -0.2, 0.2)), 0.05, 2.0)
    left_candidates = normal_values(streams_of[3], (N_DP, N_TENSOR, LB, LB), LB ** -0.5, 0.1875, ((0, 64), (1, 4)))
    right_candidates = normal_values(streams_of[4], (N_DP, N_TENSOR, RB, RB), RB ** -0.5, 0.25, ((0, 64), (1, 4)))
    left_owner = with_ends(jax.random.randint(streams_of[5], (NRB,), 0, GROUP * N_TENSOR), jax.random.fold_in(streams_of[5], 1), 0, (GROUP * N_TENSOR) - 1).astype(jnp.int32)
    right_owner = draw_right_owner(jax.random.fold_in(streams_of[7], 71), 0)
    return {"gradient": gradient, "first_moment": first_moment, "second_moment": second_moment, "left_candidates": left_candidates, "right_candidates": right_candidates, "left_owner": left_owner, "right_owner": right_owner}


beta_first = 0.9
beta_second = 0.95
correct_first = 1.0 - 0.9 ** 10
correct_second = 1.0 - 0.95 ** 10
epsilon = 1e-08

def forward_turn(matrix, right_bases, left_bases):
    blocks = matrix.reshape(N_TENSOR * CB_DEV, RB, D).astype(jnp.float32)
    turned = jnp.einsum('jpq,jpd->jqd', right_bases.astype(jnp.float32), blocks).astype(jnp.bfloat16)
    turned = turned.reshape(COLS, NRB, LB).astype(jnp.float32)
    rotated = jnp.einsum('cik,ikl->cil', turned, left_bases.astype(jnp.float32))
    return rotated.reshape(COLS, D)

def reference(gradient, first_moment, second_moment, left_candidates, right_candidates, left_owner, right_owner):
    moment_new = beta_first * first_moment + (1.0 - beta_first) * gradient.astype(jnp.float32)
    tensor_index = jnp.arange(N_TENSOR, dtype=jnp.int32)[:, None]
    right_bases = right_candidates[right_owner, tensor_index].reshape(N_TENSOR * CB_DEV, RB, RB)
    block_index = jnp.arange(NRB, dtype=jnp.int32)
    owner_dp = (block_index * GROUP + left_owner // N_TENSOR).astype(jnp.int32)
    owner_tensor = (left_owner % N_TENSOR).astype(jnp.int32)
    left_bases = left_candidates[owner_dp, owner_tensor]
    g_rot = forward_turn(gradient, right_bases, left_bases)
    m_rot = forward_turn(moment_new.astype(jnp.bfloat16), right_bases, left_bases)
    second_new = beta_second * second_moment + (1.0 - beta_second) * g_rot * g_rot
    step = (m_rot / correct_first / (jnp.sqrt(second_new / correct_second) + epsilon)).astype(jnp.bfloat16)
    step_blocks = step.reshape(COLS, NRB, LB).astype(jnp.float32)
    image = jnp.einsum('cil,ikl->cik', step_blocks, left_bases.astype(jnp.float32)).astype(jnp.bfloat16)
    image = image.reshape(N_TENSOR * CB_DEV, RB, D).astype(jnp.float32)
    update = jnp.einsum('jpq,jqd->jpd', right_bases.astype(jnp.float32), image).astype(jnp.bfloat16)
    return (moment_new, second_new, update.reshape(COLS, D))
```

```python
import jax
import jax.numpy as jnp
from jax import lax
from jax.experimental import pallas as pl
from jax.experimental.pallas import tpu as pltpu
from jax.sharding import PartitionSpec as P

MESH = pl.DeviceIdType.MESH
beta_first = 0.9
beta_second = 0.95
correct_first = 1.0 - 0.9**10
correct_second = 1.0 - 0.95**10
epsilon = 1e-08


def flip4(x, a):
    if a == 0:
        return x
    if a == 1:
        return x + 1 - 2 * (x % 2)
    if a == 2:
        return (x + 2) % 4
    return 3 - x


def kernel(
    grad, first, second, lcand, rcand, lown, rown,
    grot_out, upd_out,
    g_strip, f_strip, s_strip, m_send, s_send,
    g_in, m_in, s_in,
    l_core, l_half, l_y, l_quar, l_x, l_z, l_all,
    r_one, r_slot, r_pair, r_half, r_ring, r_part, r_cols, r_all,
    t_g, t_m, gsq, stp, g_send, u_send,
    send_sem, recv_sem, load_sem,
):
    dp, tn = lax.axis_index("dp"), lax.axis_index("tensor")
    ylo, z, x = dp // 32, (dp // 4) % 8, dp % 4
    yhi, core = tn // 2, tn % 2
    zlo = z % 2
    p = zlo * 4 + x
    group = dp // 8

    def dev(ylo_=None, z_=None, x_=None, yhi_=None, core_=None):
        a = ylo if ylo_ is None else ylo_
        b = z if z_ is None else z_
        c = x if x_ is None else x_
        d = yhi if yhi_ is None else yhi_
        e = core if core_ is None else core_
        return (a * 32 + b * 4 + c, d * 2 + e)

    zpair = z + 1 - 2 * zlo

    def in_group(r):
        return dev(x_=flip4(x, r % 4), z_=zpair if r >= 4 else z)

    def group_place(r):
        return (1 - zlo if r >= 4 else zlo) * 4 + flip4(x, r % 4)

    def in_plane(r):
        return dev(x_=flip4(x, r % 4), ylo_=1 - ylo if r >= 4 else ylo)

    def plane_place(r):
        return (1 - ylo if r >= 4 else ylo) * 4 + flip4(x, r % 4)

    count = [0]

    def remote(src, dst, to):
        i = count[0]
        count[0] += 1
        c = pltpu.make_async_remote_copy(
            src_ref=src, dst_ref=dst, send_sem=send_sem.at[i], recv_sem=recv_sem.at[i],
            device_id=to, device_id_type=MESH,
        )
        c.start()
        return c

    lcount = [0]

    def local(src, dst):
        c = pltpu.make_async_copy(src, dst, load_sem.at[lcount[0]])
        lcount[0] += 1
        c.start()
        return c

    sent = []

    def arrive(copies):
        for c in copies:
            c.wait_recv()
        sent.extend(copies)

    ld_r = local(
        rcand.at[0, 0, pl.ds(pl.multiple_of((x % 2) * 256, 256), 256),
                 pl.ds(pl.multiple_of((ylo * 2 + x // 2) * 128, 128), 128)],
        r_one.at[ylo * 4 + x],
    )
    ld_l = [
        local(lcand.at[0, 0, :, pl.ds(pl.multiple_of((core * 4 + j) * 128, 128), 128)], l_core.at[core, j])
        for j in range(4)
    ]
    ld_g0 = local(grad.at[pl.ds(pl.multiple_of(p * 512, 512), 512)], g_in.at[p])
    ld_g, ld_f, ld_s = local(grad, g_strip), local(first, f_strip), local(second, s_strip)

    peers = [in_group(r) for r in range(1, 8)]
    peers += [in_plane(r) for r in range(4, 8)]
    peers += [dev(z_=(z + r) % 8) for r in range(2, 7)]
    peers += [dev(z_=(z + 7 + 2 * zlo) % 8)]
    peers += [dev(yhi_=1 - yhi), dev(core_=1 - core)]
    barrier = pltpu.get_barrier_semaphore()
    for to in peers:
        pl.semaphore_signal(barrier, inc=1, device_id=to, device_id_type=MESH)
    pl.semaphore_wait(barrier, len(peers))

    lo = lown[group]
    o_core, o_yhi, o_x, o_zlo = lo % 2, (lo // 2) % 2, (lo // 4) % 4, lo // 16

    def right(slot):
        d = rown[0, (slot % 2) * 4 + slot // 2]
        return d // 32, (d // 4) % 8, d % 4

    l1 = [
        remote(
            lcand.at[0, 0, :, pl.ds(pl.multiple_of(((1 - core) * 4 + j) * 128, 128), 128)],
            l_core.at[core, j], dev(core_=1 - core),
        )
        for j in range(4)
    ]
    r1 = []
    for r in range(1, 8):
        q = plane_place(r)
        r1.append(remote(
            rcand.at[0, 0, pl.ds(pl.multiple_of((q % 2) * 256, 256), 256),
                     pl.ds(pl.multiple_of((q // 2) * 128, 128), 128)],
            r_one.at[ylo * 4 + x], in_plane(r),
        ))

    def spread(src, dst):
        out = []
        for r in range(1, 8):
            q = group_place(r)
            out.append(remote(src.at[pl.ds(pl.multiple_of(q * 512, 512), 512)], dst.at[p], in_group(r)))
        return out

    a_g = spread(grad, g_in)

    for c in ld_l:
        c.wait()
    arrive(l1)
    l_half[...] = l_core[o_core]
    l2 = [remote(l_half.at[pl.ds((1 - yhi) * 2, 2)], l_y.at[yhi], dev(yhi_=1 - yhi))]
    l_y[yhi] = l_half[pl.ds(yhi * 2, 2)]

    ld_g.wait()
    ld_f.wait()

    def fold(i, carry):
        rows = pl.ds(pl.multiple_of(i * 256, 256), 256)
        m_send[rows] = (
            beta_first * f_strip[rows] + (1.0 - beta_first) * g_strip[rows].astype(jnp.float32)
        ).astype(jnp.bfloat16)
        return carry

    lax.fori_loop(0, 16, fold, 0)
    a_m = spread(m_send, m_in)
    m_in[p] = m_send[pl.ds(pl.multiple_of(p * 512, 512), 512)]

    ld_r.wait()
    arrive(r1)
    for s in range(8):
        oy, oz, ox = right(s)
        r_slot[s] = r_one[oy * 4 + ox]
    r2 = [remote(
        r_slot.at[:, pl.ds(pl.multiple_of((1 - zlo) * 128, 128), 128)], r_pair.at[zlo],
        dev(z_=(z + 7 + 2 * zlo) % 8),
    )]
    r_pair[zlo] = r_slot[:, pl.ds(pl.multiple_of(zlo * 128, 128), 128)]

    ld_s.wait()

    def narrow(i, carry):
        rows = pl.ds(pl.multiple_of(i * 256, 256), 256)
        s_send[rows] = s_strip[rows].astype(jnp.bfloat16)
        return carry

    lax.fori_loop(0, 16, narrow, 0)
    s_in[p] = s_send[pl.ds(pl.multiple_of(p * 512, 512), 512)]

    arrive(r2)
    for s in range(8):
        oy, oz, ox = right(s)
        r_half[s] = r_pair[oz % 2, s]
    ring = ((z + 1) // 2) % 4
    r3 = [
        remote(
            r_half.at[:, pl.ds(pl.multiple_of(((ring + r) % 4) * 32, 32), 32)], r_ring.at[ring],
            dev(z_=(z + 2 * r) % 8),
        )
        for r in range(1, 4)
    ]
    r_ring[ring] = r_half[:, pl.ds(pl.multiple_of(ring * 32, 32), 32)]

    arrive(l2)
    for i in range(4):
        l_quar[i] = l_y[o_yhi, i // 2, (i % 2) * 512:(i % 2) * 512 + 512]
    l3 = [remote(l_quar.at[flip4(x, r)], l_x.at[x], dev(x_=flip4(x, r))) for r in range(1, 4)]
    l_x[x] = l_quar[x]

    arrive(r3)
    for s in range(8):
        oy, oz, ox = right(s)
        r_part[s // 2, s % 2] = r_ring[((oz + 1) // 2) % 4, s]
    r4 = [remote(r_part.at[flip4(x, r)], r_cols.at[x], dev(x_=flip4(x, r))) for r in range(1, 4)]
    r_cols[x] = r_part[x]

    a_s = spread(s_send, s_in)

    arrive(r4)
    sub = zlo * 4 + ring
    r5 = [
        remote(
            r_cols.at[:, (z + r) % 2], r_all.at[pl.ds(ylo * 4, 4), sub], dev(z_=(z + r) % 8),
        )
        for r in range(1, 8)
    ]
    r_all[pl.ds(ylo * 4, 4), sub] = r_cols[:, zlo]

    arrive(l3)
    l_z[zlo] = l_x[o_x]
    l4 = [remote(l_z.at[zlo], l_z.at[zlo], dev(z_=zpair))]
    arrive(l4)
    place = core * 8 + yhi * 4 + x
    l_all[place] = l_z[o_zlo]
    l5 = [remote(l_all.at[place], l_all.at[place], dev(x_=flip4(x, r))) for r in range(1, 4)]

    arrive(r5)
    r6 = [remote(r_all.at[pl.ds(ylo * 4, 4)], r_all.at[pl.ds(ylo * 4, 4)], dev(ylo_=1 - ylo))]

    arrive(l5)
    mine = pl.ds(core * 8 + yhi * 4, 4)
    l6 = [remote(l_all.at[mine], l_all.at[mine], dev(yhi_=1 - yhi))]

    arrive(r6)

    def right_basis():
        return jnp.concatenate([r_all[2 * j:2 * j + 2].reshape(512, 128) for j in range(4)], axis=1)

    def turn(src, dst):
        basis = right_basis()

        def one(j, carry):
            cols = jnp.concatenate([src[2 * j], src[2 * j + 1]], axis=1)
            t = lax.dot_general(basis, cols, (((0,), (0,)), ((), ())), preferred_element_type=jnp.float32)
            dst[:, pl.ds(pl.multiple_of(j * 256, 256), 256)] = t.astype(jnp.bfloat16)
            return carry

        lax.fori_loop(0, 4, one, 0)

    ld_g0.wait()
    arrive(a_g)
    turn(g_in, t_g)
    arrive(a_m)
    turn(m_in, t_m)

    arrive(l6)
    l7 = [remote(l_all.at[pl.ds(core * 8, 8)], l_all.at[pl.ds(core * 8, 8)], dev(core_=1 - core))]
    arrive(l7)

    def pair_at(s):
        return (1 - zlo if s >= 2 else zlo) * 2 + (1 - x // 2 if s % 2 else x // 2)

    def left_cols(j):
        return jnp.concatenate(
            [l_all[pl.ds(4 * j, 2)].reshape(1024, 128), l_all[pl.ds(4 * j + 2, 2)].reshape(1024, 128)], axis=1
        )

    home = pl.ds(pl.multiple_of(p * 512, 512), 512)
    back = []

    def send_home(buf, out, s):
        for r in (2 * s, 2 * s + 1):
            q = group_place(r)
            if r == 0:
                back_local.append(local(buf.at[q], out.at[home]))
            else:
                back.append(remote(buf.at[q], out.at[home], in_group(r)))

    back_local = []
    for s in range(4):
        j = pair_at(s)
        g = jnp.dot(t_g[...], left_cols(j), preferred_element_type=jnp.float32)
        gsq[j] = g * g
        low = g.astype(jnp.bfloat16)
        g_send[2 * j] = low[:, :128]
        g_send[2 * j + 1] = low[:, 128:]
        send_home(g_send, grot_out, s)

    arrive(a_s)

    def left_moment(j, carry):
        m = jnp.dot(t_m[...], left_cols(j), preferred_element_type=jnp.float32)
        old = jnp.concatenate([s_in[2 * j], s_in[2 * j + 1]], axis=1).astype(jnp.float32)
        new = beta_second * old + (1.0 - beta_second) * gsq[j]
        step = m / (correct_first * (jnp.sqrt(new * (1.0 / correct_second)) + epsilon))
        stp[:, pl.ds(pl.multiple_of(j * 256, 256), 256)] = step.astype(jnp.bfloat16)
        return carry

    lax.fori_loop(0, 4, left_moment, 0)

    for s in range(4):
        j = pair_at(s)
        half = j // 2
        start = pl.ds(pl.multiple_of((j % 2) * 256, 256), 256)
        rows = jnp.concatenate([l_all[2 * b + half, start] for b in range(8)], axis=1)
        image = lax.dot_general(
            stp[...], rows, (((1,), (1,)), ((), ())), preferred_element_type=jnp.float32
        ).astype(jnp.bfloat16)
        out = jnp.dot(right_basis(), image, preferred_element_type=jnp.float32).astype(jnp.bfloat16)
        u_send[2 * j] = out[:, :128]
        u_send[2 * j + 1] = out[:, 128:]
        send_home(u_send, upd_out, s)

    arrive(back)
    for c in back_local:
        c.wait()
    for c in sent:
        c.wait_send()


def body(gradient, first_moment, second_moment, left_candidates, right_candidates, left_owner, right_owner):
    bf, f32 = jnp.bfloat16, jnp.float32
    any_, smem = pl.BlockSpec(memory_space=pl.ANY), pl.BlockSpec(memory_space=pltpu.SMEM)
    vm = pltpu.VMEM
    strip = jax.ShapeDtypeStruct(gradient.shape, bf)
    grot, update = pl.pallas_call(
        kernel,
        name="soap_swap",
        out_shape=(strip, strip),
        in_specs=[any_] * 5 + [smem] * 2,
        out_specs=(any_, any_),
        scratch_shapes=[
            vm((4096, 128), bf), vm((4096, 128), f32), vm((4096, 128), f32), vm((4096, 128), bf), vm((4096, 128), bf),
            vm((8, 512, 128), bf), vm((8, 512, 128), bf), vm((8, 512, 128), bf),
            vm((2, 4, 1024, 128), bf), vm((4, 1024, 128), bf), vm((2, 2, 1024, 128), bf),
            vm((4, 512, 128), bf), vm((4, 512, 128), bf), vm((2, 512, 128), bf), vm((16, 512, 128), bf),
            vm((8, 256, 128), bf), vm((8, 256, 128), bf), vm((2, 8, 128, 128), bf), vm((8, 128, 128), bf),
            vm((4, 8, 32, 128), bf), vm((4, 2, 32, 128), bf), vm((4, 2, 32, 128), bf), vm((8, 8, 32, 128), bf),
            vm((512, 1024), bf), vm((512, 1024), bf), vm((4, 512, 256), f32), vm((512, 1024), bf),
            vm((8, 512, 128), bf), vm((8, 512, 128), bf),
            pltpu.SemaphoreType.DMA((72,)), pltpu.SemaphoreType.DMA((72,)), pltpu.SemaphoreType.DMA((16,)),
        ],
        compiler_params=pltpu.CompilerParams(
            collective_id=0, has_side_effects=True, vmem_limit_bytes=56 * 2**20
        ),
    )(gradient, first_moment, second_moment, left_candidates, right_candidates, left_owner, right_owner)
    moment_new = beta_first * first_moment + (1.0 - beta_first) * gradient.astype(f32)
    turned = grot.astype(f32)
    second_new = beta_second * second_moment + (1.0 - beta_second) * turned * turned
    return moment_new, second_new, update


def solution(mesh):
    strips = P("tensor", "dp")
    placed = (strips, strips, strips, P("dp", "tensor", None, None), P("dp", "tensor", None, None), P(), P("tensor", None))
    return jax.shard_map(body, mesh=mesh, in_specs=placed, out_specs=(strips,) * 3, check_vma=False)
```

```python
import jax
import jax.numpy as jnp
from jax import lax
from jax.experimental import pallas as pl
from jax.experimental.pallas import tpu as pltpu
from jax.sharding import PartitionSpec as P

MESH = pl.DeviceIdType.MESH
beta_first = 0.9
beta_second = 0.95
correct_first = 1.0 - 0.9**10
correct_second = 1.0 - 0.95**10
epsilon = 1e-08

ORDER = "PgBsQggmmPBggmAQPgABPQAmBPBAQPgABmQssmAsQsPsmsBAQABGhhhShMwuuuu"


def flip4(x, a):
    if a == 0:
        return x
    if a == 1:
        return x + 1 - 2 * (x % 2)
    if a == 2:
        return (x + 2) % 4
    return 3 - x


def kernel(
    grad, first, second, lcand, rcand, lown, rown,
    grot_out, upd_out,
    g_strip, f_strip, s_strip, m_send, s_send,
    g_in, m_in, s_in,
    l_half, l_quar, l_all, r_slot, r_half, r_part, r_cols, r_all,
    l_core0, l_core1, l_y0, l_y1, l_x0, l_x1, l_z0, l_z1, r_one0, r_one1, r_pair0, r_pair1, r_ring0, r_ring1,
    t_g, t_m, gsq, stp, g_send, u_send,
    send_sem, recv_sem, load_sem,
):
    dp, tn = lax.axis_index("dp"), lax.axis_index("tensor")
    ylo, z, x = dp // 32, (dp // 4) % 8, dp % 4
    yhi, core = tn // 2, tn % 2
    zlo = z % 2
    l_core, l_y, l_x, l_z = (l_core0, l_core1), (l_y0, l_y1), (l_x0, l_x1), (l_z0, l_z1)
    r_one, r_pair, r_ring = (r_one0, r_one1), (r_pair0, r_pair1), (r_ring0, r_ring1)
    p = zlo * 4 + x
    group = dp // 8

    def dev(ylo_=None, z_=None, x_=None, yhi_=None, core_=None):
        a = ylo if ylo_ is None else ylo_
        b = z if z_ is None else z_
        c = x if x_ is None else x_
        d = yhi if yhi_ is None else yhi_
        e = core if core_ is None else core_
        return (a * 32 + b * 4 + c, d * 2 + e)

    zpair = z + 1 - 2 * zlo

    def in_group(r):
        return dev(x_=flip4(x, r % 4), z_=zpair if r >= 4 else z)

    def group_place(r):
        return (1 - zlo if r >= 4 else zlo) * 4 + flip4(x, r % 4)

    def in_plane(r):
        return dev(x_=flip4(x, r % 4), ylo_=1 - ylo if r >= 4 else ylo)

    def plane_place(r):
        return (1 - ylo if r >= 4 else ylo) * 4 + flip4(x, r % 4)

    count = [0]

    def remote(src, dst, to):
        i = count[0]
        count[0] += 1
        c = pltpu.make_async_remote_copy(
            src_ref=src, dst_ref=dst, send_sem=send_sem.at[i], recv_sem=recv_sem.at[i],
            device_id=to, device_id_type=MESH,
        )
        c.start()
        return c

    lcount = [0]

    def local(src, dst):
        c = pltpu.make_async_copy(src, dst, load_sem.at[lcount[0]])
        lcount[0] += 1
        c.start()
        return c

    sent = []

    def arrive(copies):
        for c in copies:
            c.wait_recv()
        sent.extend(copies)

    ld_r = [
        local(
            rcand.at[0, 0, pl.ds(pl.multiple_of((x % 2) * 256 + h * 128, 128), 128),
                     pl.ds(pl.multiple_of((ylo * 2 + x // 2) * 128, 128), 128)],
            r_one[h].at[ylo * 4 + x],
        )
        for h in range(2)
    ]
    ld_l = [
        [
            local(
                lcand.at[0, 0, pl.ds(h * 512, 512), pl.ds(pl.multiple_of((core * 4 + j) * 128, 128), 128)],
                l_core[h].at[core, j],
            )
            for j in range(4)
        ]
        for h in range(2)
    ]
    ld_g0 = local(grad.at[pl.ds(pl.multiple_of(p * 512, 512), 512)], g_in.at[p])
    ld_g, ld_f, ld_s = local(grad, g_strip), local(first, f_strip), local(second, s_strip)

    peers = [in_group(r) for r in range(1, 8)]
    peers += [in_plane(r) for r in range(4, 8)]
    peers += [dev(z_=(z + r) % 8) for r in range(2, 7)]
    peers += [dev(z_=(z + 7 + 2 * zlo) % 8)]
    peers += [dev(yhi_=1 - yhi), dev(core_=1 - core)]
    barrier = pltpu.get_barrier_semaphore()
    for to in peers:
        pl.semaphore_signal(barrier, inc=1, device_id=to, device_id_type=MESH)
    pl.semaphore_wait(barrier, len(peers))

    lo = lown[group]
    o_core, o_yhi, o_x, o_zlo = lo % 2, (lo // 2) % 2, (lo // 4) % 4, lo // 16

    def right(slot):
        d = rown[0, (slot % 2) * 4 + slot // 2]
        return d // 32, (d // 4) % 8, d % 4

    def spread(src, dst, wait):
        for r in (4, 1, 3, 2, 5, 7, 6):
            q = group_place(r)
            wait.append(remote(src.at[pl.ds(pl.multiple_of(q * 512, 512), 512)], dst.at[p], in_group(r)))
            yield

    def left_chain(h):
        rows = pl.ds(h * 512, 512)
        wait = [
            remote(
                lcand.at[0, 0, rows, pl.ds(pl.multiple_of(((1 - core) * 4 + j) * 128, 128), 128)],
                l_core[h].at[core, j], dev(core_=1 - core),
            )
            for j in range(4)
        ]
        yield
        for c in ld_l[h]:
            c.wait()
        arrive(wait)
        l_half[h] = l_core[h][o_core]
        wait = [remote(l_half.at[h, pl.ds((1 - yhi) * 2, 2)], l_y[h].at[yhi], dev(yhi_=1 - yhi))]
        l_y[h][yhi] = l_half[h, pl.ds(yhi * 2, 2)]
        yield
        arrive(wait)
        for i in range(4):
            l_quar[h, i] = l_y[h][o_yhi, i // 2, (i % 2) * 256:(i % 2) * 256 + 256]
        wait = [remote(l_quar.at[h, flip4(x, r)], l_x[h].at[x], dev(x_=flip4(x, r))) for r in range(1, 4)]
        l_x[h][x] = l_quar[h, x]
        yield
        arrive(wait)
        l_z[h][zlo] = l_x[h][o_x]
        wait = [remote(l_z[h].at[zlo], l_z[h].at[zlo], dev(z_=zpair))]
        yield
        arrive(wait)
        mine = l_all.at[core * 4 + yhi * 2 + x // 2, h, x % 2]
        mine[...] = l_z[h][o_zlo]
        wait = [remote(mine, mine, dev(x_=flip4(x, r))) for r in range(1, 4)]
        yield
        arrive(wait)
        mine = l_all.at[pl.ds(core * 4 + yhi * 2, 2), h]
        wait = [remote(mine, mine, dev(yhi_=1 - yhi))]
        yield
        arrive(wait)
        mine = l_all.at[pl.ds(core * 4, 4), h]
        wait = [remote(mine, mine, dev(core_=1 - core))]
        yield
        arrive(wait)
        yield

    def right_chain(h):
        wait = []
        for r in range(1, 8):
            q = plane_place(r)
            wait.append(remote(
                rcand.at[0, 0, pl.ds(pl.multiple_of((q % 2) * 256 + h * 128, 128), 128),
                         pl.ds(pl.multiple_of((q // 2) * 128, 128), 128)],
                r_one[h].at[ylo * 4 + x], in_plane(r),
            ))
        yield
        ld_r[h].wait()
        arrive(wait)
        for s in range(8):
            oy, oz, ox = right(s)
            r_slot[h, s] = r_one[h][oy * 4 + ox]
        wait = [remote(
            r_slot.at[h, :, pl.ds(pl.multiple_of((1 - zlo) * 64, 64), 64)], r_pair[h].at[zlo],
            dev(z_=(z + 7 + 2 * zlo) % 8),
        )]
        r_pair[h][zlo] = r_slot[h, :, pl.ds(pl.multiple_of(zlo * 64, 64), 64)]
        yield
        arrive(wait)
        for s in range(8):
            oy, oz, ox = right(s)
            r_half[h, s] = r_pair[h][oz % 2, s]
        ring = ((z + 1) // 2) % 4
        wait = [
            remote(
                r_half.at[h, :, pl.ds(pl.multiple_of(((ring + r) % 4) * 16, 16), 16)], r_ring[h].at[ring],
                dev(z_=(z + 2 * r) % 8),
            )
            for r in range(1, 4)
        ]
        r_ring[h][ring] = r_half[h, :, pl.ds(pl.multiple_of(ring * 16, 16), 16)]
        yield
        arrive(wait)
        for s in range(8):
            oy, oz, ox = right(s)
            r_part[h, s // 2, s % 2] = r_ring[h][((oz + 1) // 2) % 4, s]
        wait = [remote(r_part.at[h, flip4(x, r)], r_cols.at[h, x], dev(x_=flip4(x, r))) for r in range(1, 4)]
        r_cols[h, x] = r_part[h, x]
        yield
        arrive(wait)
        sub = zlo * 4 + ring
        wait = [
            remote(
                r_cols.at[h, :, (z + r) % 2], r_all.at[pl.ds(ylo * 4, 4), h, sub], dev(z_=(z + r) % 8),
            )
            for r in range(1, 8)
        ]
        r_all[pl.ds(ylo * 4, 4), h, sub] = r_cols[h, :, zlo]
        yield
        arrive(wait)
        mine = r_all.at[pl.ds(ylo * 4, 4), h]
        wait = [remote(mine, mine, dev(ylo_=1 - ylo))]
        yield
        arrive(wait)
        yield

    def right_basis():
        return jnp.concatenate([r_all[2 * j:2 * j + 2].reshape(512, 128) for j in range(4)], axis=1)

    def turn(src, dst):
        basis = right_basis()

        def one(j, carry):
            cols = jnp.concatenate([src[2 * j], src[2 * j + 1]], axis=1)
            t = lax.dot_general(basis, cols, (((0,), (0,)), ((), ())), preferred_element_type=jnp.float32)
            dst[:, pl.ds(pl.multiple_of(j * 256, 256), 256)] = t.astype(jnp.bfloat16)
            return carry

        lax.fori_loop(0, 4, one, 0)

    def gradient_chain():
        wait = []
        yield from spread(grad, g_in, wait)
        ld_g0.wait()
        arrive(wait)
        turn(g_in, t_g)
        yield

    def moment_chain():
        ld_g.wait()
        ld_f.wait()

        def fold(i, carry):
            rows = pl.ds(pl.multiple_of(i * 256, 256), 256)
            m_send[rows] = (
                beta_first * f_strip[rows] + (1.0 - beta_first) * g_strip[rows].astype(jnp.float32)
            ).astype(jnp.bfloat16)
            return carry

        lax.fori_loop(0, 16, fold, 0)
        m_in[p] = m_send[pl.ds(pl.multiple_of(p * 512, 512), 512)]
        wait = []
        yield from spread(m_send, m_in, wait)
        arrive(wait)
        turn(m_in, t_m)
        yield

    def second_chain():
        ld_s.wait()

        def narrow(i, carry):
            rows = pl.ds(pl.multiple_of(i * 256, 256), 256)
            s_send[rows] = s_strip[rows].astype(jnp.bfloat16)
            return carry

        lax.fori_loop(0, 16, narrow, 0)
        s_in[p] = s_send[pl.ds(pl.multiple_of(p * 512, 512), 512)]
        wait = []
        yield from spread(s_send, s_in, wait)
        arrive(wait)
        yield

    def pair_at(s):
        return (1 - zlo if s >= 2 else zlo) * 2 + (1 - x // 2 if s % 2 else x // 2)

    def left_cols(j):
        return jnp.concatenate(
            [l_all[2 * j].reshape(1024, 128), l_all[2 * j + 1].reshape(1024, 128)], axis=1
        )

    home = pl.ds(pl.multiple_of(p * 512, 512), 512)
    back, back_local = [], []

    def send_home(buf, out, s):
        for r in (2 * s, 2 * s + 1):
            q = group_place(r)
            if r == 0:
                back_local.append(local(buf.at[q], out.at[home]))
            else:
                back.append(remote(buf.at[q], out.at[home], in_group(r)))

    def home_gradient():
        for s in range(4):
            j = pair_at(s)
            g = jnp.dot(t_g[...], left_cols(j), preferred_element_type=jnp.float32)
            gsq[j] = g * g
            low = g.astype(jnp.bfloat16)
            g_send[2 * j] = low[:, :128]
            g_send[2 * j + 1] = low[:, 128:]
            send_home(g_send, grot_out, s)
            yield

    def make_step():
        def left_moment(j, carry):
            m = jnp.dot(t_m[...], left_cols(j), preferred_element_type=jnp.float32)
            old = jnp.concatenate([s_in[2 * j], s_in[2 * j + 1]], axis=1).astype(jnp.float32)
            new = beta_second * old + (1.0 - beta_second) * gsq[j]
            step = m / (correct_first * (jnp.sqrt(new * (1.0 / correct_second)) + epsilon))
            stp[:, pl.ds(pl.multiple_of(j * 256, 256), 256)] = step.astype(jnp.bfloat16)
            return carry

        lax.fori_loop(0, 4, left_moment, 0)
        yield

    def home_update():
        for s in range(4):
            j = pair_at(s)
            rows = jnp.concatenate([l_all[b, j // 2, j % 2] for b in range(8)], axis=1)
            image = lax.dot_general(
                stp[...], rows, (((1,), (1,)), ((), ())), preferred_element_type=jnp.float32
            ).astype(jnp.bfloat16)
            out = jnp.dot(right_basis(), image, preferred_element_type=jnp.float32).astype(jnp.bfloat16)
            u_send[2 * j] = out[:, :128]
            u_send[2 * j + 1] = out[:, 128:]
            send_home(u_send, upd_out, s)
            yield

    g, m, s = gradient_chain(), moment_chain(), second_chain()
    chains = {
        "A": left_chain(0), "B": left_chain(1), "P": right_chain(0), "Q": right_chain(1),
        "g": g, "G": g, "m": m, "M": m, "s": s, "S": s,
        "h": home_gradient(), "w": make_step(), "u": home_update(),
    }
    for name in ORDER:
        next(chains[name])

    arrive(back)
    for c in back_local:
        c.wait()
    for c in sent:
        c.wait_send()


def body(gradient, first_moment, second_moment, left_candidates, right_candidates, left_owner, right_owner):
    bf, f32 = jnp.bfloat16, jnp.float32
    any_, smem = pl.BlockSpec(memory_space=pl.ANY), pl.BlockSpec(memory_space=pltpu.SMEM)
    vm = pltpu.VMEM
    strip = jax.ShapeDtypeStruct(gradient.shape, bf)
    grot, update = pl.pallas_call(
        kernel,
        name="soap_swap",
        out_shape=(strip, strip),
        in_specs=[any_] * 5 + [smem] * 2,
        out_specs=(any_, any_),
        scratch_shapes=[
            vm((4096, 128), bf), vm((4096, 128), f32), vm((4096, 128), f32), vm((4096, 128), bf), vm((4096, 128), bf),
            vm((8, 512, 128), bf), vm((8, 512, 128), bf), vm((8, 512, 128), bf),
            vm((2, 4, 512, 128), bf), vm((2, 4, 256, 128), bf), vm((8, 2, 2, 256, 128), bf),
            vm((2, 8, 128, 128), bf), vm((2, 8, 64, 128), bf), vm((2, 4, 2, 16, 128), bf), vm((2, 4, 2, 16, 128), bf),
            vm((8, 2, 8, 16, 128), bf),
            *[vm((2, 4, 512, 128), bf)] * 2, *[vm((2, 2, 512, 128), bf)] * 2,
            *[vm((4, 256, 128), bf)] * 2, *[vm((2, 256, 128), bf)] * 2,
            *[vm((8, 128, 128), bf)] * 2, *[vm((2, 8, 64, 128), bf)] * 2, *[vm((4, 8, 16, 128), bf)] * 2,
            vm((512, 1024), bf), vm((512, 1024), bf), vm((4, 512, 256), f32), vm((512, 1024), bf),
            vm((8, 512, 128), bf), vm((8, 512, 128), bf),
            pltpu.SemaphoreType.DMA((112,)), pltpu.SemaphoreType.DMA((112,)), pltpu.SemaphoreType.DMA((24,)),
        ],
        compiler_params=pltpu.CompilerParams(
            collective_id=0, has_side_effects=True, vmem_limit_bytes=56 * 2**20
        ),
    )(gradient, first_moment, second_moment, left_candidates, right_candidates, left_owner, right_owner)
    moment_new = beta_first * first_moment + (1.0 - beta_first) * gradient.astype(f32)
    turned = grot.astype(f32)
    second_new = beta_second * second_moment + (1.0 - beta_second) * turned * turned
    return moment_new, second_new, update


def solution(mesh):
    strips = P("tensor", "dp")
    placed = (strips, strips, strips, P("dp", "tensor", None, None), P("dp", "tensor", None, None), P(), P("tensor", None))
    return jax.shard_map(body, mesh=mesh, in_specs=placed, out_specs=(strips,) * 3, check_vma=False)
```

```python
import jax
import jax.numpy as jnp
from jax import lax
from jax.experimental import pallas as pl
from jax.experimental.pallas import tpu as pltpu
from jax.sharding import PartitionSpec as P

MESH = pl.DeviceIdType.MESH
beta_first = 0.9
beta_second = 0.95
correct_first = 1.0 - 0.9**10
correct_second = 1.0 - 0.95**10
epsilon = 1e-08

ORDER = "PQssgAggBgBPggsAQPmQBPABsPBQAssPAmgBmPmQ" + "AsmmQBABmQGAhhShMhwuuuu"


def flip4(x, a):
    if a == 0:
        return x
    if a == 1:
        return x + 1 - 2 * (x % 2)
    if a == 2:
        return (x + 2) % 4
    return 3 - x


def kernel(
    grad, first, second, lcand, rcand, lown, rown,
    grot_out, upd_out,
    g_strip, f_strip, s_strip, m_send, s_send,
    g_in, m_in, s_in,
    l_half, l_quar, l_all, r_slot, r_half, r_part, r_cols, r_all,
    l_core0, l_core1, l_y0, l_y1, l_x0, l_x1, l_z0, l_z1, r_one0, r_one1, r_pair0, r_pair1, r_ring0, r_ring1,
    t_g, t_m, gsq, stp, g_send, u_send,
    send_sem, recv_sem, load_sem,
):
    dp, tn = lax.axis_index("dp"), lax.axis_index("tensor")
    ylo, z, x = dp // 32, (dp // 4) % 8, dp % 4
    yhi, core = tn // 2, tn % 2
    zlo = z % 2
    l_core, l_y, l_x, l_z = (l_core0, l_core1), (l_y0, l_y1), (l_x0, l_x1), (l_z0, l_z1)
    r_one, r_pair, r_ring = (r_one0, r_one1), (r_pair0, r_pair1), (r_ring0, r_ring1)
    p = zlo * 4 + x
    group = dp // 8

    def dev(ylo_=None, z_=None, x_=None, yhi_=None, core_=None):
        a = ylo if ylo_ is None else ylo_
        b = z if z_ is None else z_
        c = x if x_ is None else x_
        d = yhi if yhi_ is None else yhi_
        e = core if core_ is None else core_
        return (a * 32 + b * 4 + c, d * 2 + e)

    zpair = z + 1 - 2 * zlo

    def in_group(r):
        return dev(x_=flip4(x, r % 4), z_=zpair if r >= 4 else z)

    def group_place(r):
        return (1 - zlo if r >= 4 else zlo) * 4 + flip4(x, r % 4)

    def in_plane(r):
        return dev(x_=flip4(x, r % 4), ylo_=1 - ylo if r >= 4 else ylo)

    def plane_place(r):
        return (1 - ylo if r >= 4 else ylo) * 4 + flip4(x, r % 4)

    count = [0]

    def remote(src, dst, to):
        i = count[0]
        count[0] += 1
        c = pltpu.make_async_remote_copy(
            src_ref=src, dst_ref=dst, send_sem=send_sem.at[i], recv_sem=recv_sem.at[i],
            device_id=to, device_id_type=MESH,
        )
        c.start()
        return c

    lcount = [0]

    def local(src, dst):
        c = pltpu.make_async_copy(src, dst, load_sem.at[lcount[0]])
        lcount[0] += 1
        c.start()
        return c

    sent = []

    def arrive(copies):
        for c in copies:
            c.wait_recv()
        sent.extend(copies)

    ld_r = [
        local(
            rcand.at[0, 0, pl.ds(pl.multiple_of((x % 2) * 256 + h * 128, 128), 128),
                     pl.ds(pl.multiple_of((ylo * 2 + x // 2) * 128, 128), 128)],
            r_one[h].at[ylo * 4 + x],
        )
        for h in range(2)
    ]
    ld_l = [
        [
            local(
                lcand.at[0, 0, pl.ds(h * 512, 512), pl.ds(pl.multiple_of((core * 4 + j) * 128, 128), 128)],
                l_core[h].at[core, j],
            )
            for j in range(4)
        ]
        for h in range(2)
    ]
    ld_g0 = local(grad.at[pl.ds(pl.multiple_of(p * 512, 512), 512)], g_in.at[p])
    ld_g, ld_f, ld_s = local(grad, g_strip), local(first, f_strip), local(second, s_strip)

    peers = [in_group(r) for r in range(1, 8)]
    peers += [in_plane(r) for r in range(4, 8)]
    peers += [dev(z_=(z + r) % 8) for r in range(2, 7)]
    peers += [dev(z_=(z + 7 + 2 * zlo) % 8)]
    peers += [dev(yhi_=1 - yhi), dev(core_=1 - core)]
    barrier = pltpu.get_barrier_semaphore()
    for to in peers:
        pl.semaphore_signal(barrier, inc=1, device_id=to, device_id_type=MESH)
    pl.semaphore_wait(barrier, len(peers))

    lo = lown[group]
    o_core, o_yhi, o_x, o_zlo = lo % 2, (lo // 2) % 2, (lo // 4) % 4, lo // 16

    def right(slot):
        d = rown[0, (slot % 2) * 4 + slot // 2]
        return d // 32, (d // 4) % 8, d % 4

    def spread(src, dst, wait):
        for r in (4, 1, 3, 2, 5, 7, 6):
            q = group_place(r)
            wait.append(remote(src.at[pl.ds(pl.multiple_of(q * 512, 512), 512)], dst.at[p], in_group(r)))
            yield

    def left_chain(h):
        rows = pl.ds(h * 512, 512)
        wait = [
            remote(
                lcand.at[0, 0, rows, pl.ds(pl.multiple_of(((1 - core) * 4 + j) * 128, 128), 128)],
                l_core[h].at[core, j], dev(core_=1 - core),
            )
            for j in range(4)
        ]
        yield
        for c in ld_l[h]:
            c.wait()
        arrive(wait)
        l_half[h] = l_core[h][o_core]
        wait = [remote(l_half.at[h, pl.ds((1 - yhi) * 2, 2)], l_y[h].at[yhi], dev(yhi_=1 - yhi))]
        l_y[h][yhi] = l_half[h, pl.ds(yhi * 2, 2)]
        yield
        arrive(wait)
        for i in range(4):
            l_quar[h, i] = l_y[h][o_yhi, i // 2, (i % 2) * 256:(i % 2) * 256 + 256]
        wait = [remote(l_quar.at[h, flip4(x, r)], l_x[h].at[x], dev(x_=flip4(x, r))) for r in range(1, 4)]
        l_x[h][x] = l_quar[h, x]
        yield
        arrive(wait)
        l_z[h][zlo] = l_x[h][o_x]
        wait = [remote(l_z[h].at[zlo], l_z[h].at[zlo], dev(z_=zpair))]
        yield
        arrive(wait)
        mine = l_all.at[core * 4 + yhi * 2 + x // 2, h, x % 2]
        mine[...] = l_z[h][o_zlo]
        wait = [remote(mine, mine, dev(x_=flip4(x, r))) for r in range(1, 4)]
        yield
        arrive(wait)
        mine = l_all.at[pl.ds(core * 4 + yhi * 2, 2), h]
        wait = [remote(mine, mine, dev(yhi_=1 - yhi))]
        yield
        arrive(wait)
        mine = l_all.at[pl.ds(core * 4, 4), h]
        wait = [remote(mine, mine, dev(core_=1 - core))]
        yield
        arrive(wait)
        yield

    def right_chain(h):
        wait = []
        for r in range(1, 8):
            q = plane_place(r)
            wait.append(remote(
                rcand.at[0, 0, pl.ds(pl.multiple_of((q % 2) * 256 + h * 128, 128), 128),
                         pl.ds(pl.multiple_of((q // 2) * 128, 128), 128)],
                r_one[h].at[ylo * 4 + x], in_plane(r),
            ))
        yield
        ld_r[h].wait()
        arrive(wait)
        for s in range(8):
            oy, oz, ox = right(s)
            r_slot[h, s] = r_one[h][oy * 4 + ox]
        wait = [remote(
            r_slot.at[h, :, pl.ds(pl.multiple_of((1 - zlo) * 64, 64), 64)], r_pair[h].at[zlo],
            dev(z_=(z + 7 + 2 * zlo) % 8),
        )]
        r_pair[h][zlo] = r_slot[h, :, pl.ds(pl.multiple_of(zlo * 64, 64), 64)]
        yield
        arrive(wait)
        for s in range(8):
            oy, oz, ox = right(s)
            r_half[h, s] = r_pair[h][oz % 2, s]
        ring = ((z + 1) // 2) % 4
        wait = [
            remote(
                r_half.at[h, :, pl.ds(pl.multiple_of(((ring + r) % 4) * 16, 16), 16)], r_ring[h].at[ring],
                dev(z_=(z + 2 * r) % 8),
            )
            for r in range(1, 4)
        ]
        r_ring[h][ring] = r_half[h, :, pl.ds(pl.multiple_of(ring * 16, 16), 16)]
        yield
        arrive(wait)
        for s in range(8):
            oy, oz, ox = right(s)
            r_part[h, s // 2, s % 2] = r_ring[h][((oz + 1) // 2) % 4, s]
        wait = [remote(r_part.at[h, flip4(x, r)], r_cols.at[h, x], dev(x_=flip4(x, r))) for r in range(1, 4)]
        r_cols[h, x] = r_part[h, x]
        yield
        arrive(wait)
        sub = zlo * 4 + ring
        wait = [
            remote(
                r_cols.at[h, :, (z + r) % 2], r_all.at[pl.ds(ylo * 4, 4), h, sub], dev(z_=(z + r) % 8),
            )
            for r in range(1, 8)
        ]
        r_all[pl.ds(ylo * 4, 4), h, sub] = r_cols[h, :, zlo]
        yield
        arrive(wait)
        mine = r_all.at[pl.ds(ylo * 4, 4), h]
        wait = [remote(mine, mine, dev(ylo_=1 - ylo))]
        yield
        arrive(wait)
        yield

    def right_basis():
        return jnp.concatenate([r_all[2 * j:2 * j + 2].reshape(512, 128) for j in range(4)], axis=1)

    def turn(src, dst):
        basis = right_basis()

        def one(j, carry):
            cols = jnp.concatenate([src[2 * j], src[2 * j + 1]], axis=1)
            t = lax.dot_general(basis, cols, (((0,), (0,)), ((), ())), preferred_element_type=jnp.float32)
            dst[:, pl.ds(pl.multiple_of(j * 256, 256), 256)] = t.astype(jnp.bfloat16)
            return carry

        lax.fori_loop(0, 4, one, 0)

    def gradient_chain():
        wait = []
        yield from spread(grad, g_in, wait)
        ld_g0.wait()
        arrive(wait)
        turn(g_in, t_g)
        yield

    def moment_chain():
        ld_g.wait()
        ld_f.wait()

        def fold(i, carry):
            rows = pl.ds(pl.multiple_of(i * 256, 256), 256)
            m_send[rows] = (
                beta_first * f_strip[rows] + (1.0 - beta_first) * g_strip[rows].astype(jnp.float32)
            ).astype(jnp.bfloat16)
            return carry

        lax.fori_loop(0, 16, fold, 0)
        m_in[p] = m_send[pl.ds(pl.multiple_of(p * 512, 512), 512)]
        wait = []
        yield from spread(m_send, m_in, wait)
        arrive(wait)
        turn(m_in, t_m)
        yield

    def second_chain():
        ld_s.wait()

        def narrow(i, carry):
            rows = pl.ds(pl.multiple_of(i * 256, 256), 256)
            s_send[rows] = s_strip[rows].astype(jnp.bfloat16)
            return carry

        lax.fori_loop(0, 16, narrow, 0)
        s_in[p] = s_send[pl.ds(pl.multiple_of(p * 512, 512), 512)]
        wait = []
        yield from spread(s_send, s_in, wait)
        arrive(wait)
        yield

    def pair_at(s):
        return (1 - zlo if s >= 2 else zlo) * 2 + (1 - x // 2 if s % 2 else x // 2)

    def left_cols(j):
        return jnp.concatenate(
            [l_all[2 * j].reshape(1024, 128), l_all[2 * j + 1].reshape(1024, 128)], axis=1
        )

    home = pl.ds(pl.multiple_of(p * 512, 512), 512)
    back, back_local = [], []

    def send_home(buf, out, s):
        for r in (2 * s, 2 * s + 1):
            q = group_place(r)
            if r == 0:
                back_local.append(local(buf.at[q], out.at[home]))
            else:
                back.append(remote(buf.at[q], out.at[home], in_group(r)))

    def home_gradient():
        for s in (2, 1, 3, 0):
            j = pair_at(s)
            g = jnp.dot(t_g[...], left_cols(j), preferred_element_type=jnp.float32)
            gsq[j] = g * g
            low = g.astype(jnp.bfloat16)
            g_send[2 * j] = low[:, :128]
            g_send[2 * j + 1] = low[:, 128:]
            send_home(g_send, grot_out, s)
            yield

    def make_step():
        def left_moment(j, carry):
            m = jnp.dot(t_m[...], left_cols(j), preferred_element_type=jnp.float32)
            old = jnp.concatenate([s_in[2 * j], s_in[2 * j + 1]], axis=1).astype(jnp.float32)
            new = beta_second * old + (1.0 - beta_second) * gsq[j]
            step = m / (correct_first * (jnp.sqrt(new * (1.0 / correct_second)) + epsilon))
            stp[:, pl.ds(pl.multiple_of(j * 256, 256), 256)] = step.astype(jnp.bfloat16)
            return carry

        lax.fori_loop(0, 4, left_moment, 0)
        yield

    def home_update():
        for s in (2, 1, 3, 0):
            j = pair_at(s)
            rows = jnp.concatenate([l_all[b, j // 2, j % 2] for b in range(8)], axis=1)
            image = lax.dot_general(
                stp[...], rows, (((1,), (1,)), ((), ())), preferred_element_type=jnp.float32
            ).astype(jnp.bfloat16)
            out = jnp.dot(right_basis(), image, preferred_element_type=jnp.float32).astype(jnp.bfloat16)
            u_send[2 * j] = out[:, :128]
            u_send[2 * j + 1] = out[:, 128:]
            send_home(u_send, upd_out, s)
            yield

    g, m, s = gradient_chain(), moment_chain(), second_chain()
    chains = {
        "A": left_chain(0), "B": left_chain(1), "P": right_chain(0), "Q": right_chain(1),
        "g": g, "G": g, "m": m, "M": m, "s": s, "S": s,
        "h": home_gradient(), "w": make_step(), "u": home_update(),
    }
    for name in ORDER:
        next(chains[name])

    arrive(back)
    for c in back_local:
        c.wait()
    for c in sent:
        c.wait_send()


def body(gradient, first_moment, second_moment, left_candidates, right_candidates, left_owner, right_owner):
    bf, f32 = jnp.bfloat16, jnp.float32
    any_, smem = pl.BlockSpec(memory_space=pl.ANY), pl.BlockSpec(memory_space=pltpu.SMEM)
    vm = pltpu.VMEM
    strip = jax.ShapeDtypeStruct(gradient.shape, bf)
    grot, update = pl.pallas_call(
        kernel,
        name="soap_swap",
        out_shape=(strip, strip),
        in_specs=[any_] * 5 + [smem] * 2,
        out_specs=(any_, any_),
        scratch_shapes=[
            vm((4096, 128), bf), vm((4096, 128), f32), vm((4096, 128), f32), vm((4096, 128), bf), vm((4096, 128), bf),
            vm((8, 512, 128), bf), vm((8, 512, 128), bf), vm((8, 512, 128), bf),
            vm((2, 4, 512, 128), bf), vm((2, 4, 256, 128), bf), vm((8, 2, 2, 256, 128), bf),
            vm((2, 8, 128, 128), bf), vm((2, 8, 64, 128), bf), vm((2, 4, 2, 16, 128), bf), vm((2, 4, 2, 16, 128), bf),
            vm((8, 2, 8, 16, 128), bf),
            *[vm((2, 4, 512, 128), bf)] * 2, *[vm((2, 2, 512, 128), bf)] * 2,
            *[vm((4, 256, 128), bf)] * 2, *[vm((2, 256, 128), bf)] * 2,
            *[vm((8, 128, 128), bf)] * 2, *[vm((2, 8, 64, 128), bf)] * 2, *[vm((4, 8, 16, 128), bf)] * 2,
            vm((512, 1024), bf), vm((512, 1024), bf), vm((4, 512, 256), f32), vm((512, 1024), bf),
            vm((8, 512, 128), bf), vm((8, 512, 128), bf),
            pltpu.SemaphoreType.DMA((112,)), pltpu.SemaphoreType.DMA((112,)), pltpu.SemaphoreType.DMA((24,)),
        ],
        compiler_params=pltpu.CompilerParams(
            collective_id=0, has_side_effects=True, vmem_limit_bytes=56 * 2**20
        ),
    )(gradient, first_moment, second_moment, left_candidates, right_candidates, left_owner, right_owner)
    moment_new = beta_first * first_moment + (1.0 - beta_first) * gradient.astype(f32)
    turned = grot.astype(f32)
    second_new = beta_second * second_moment + (1.0 - beta_second) * turned * turned
    return moment_new, second_new, update


def solution(mesh):
    strips = P("tensor", "dp")
    placed = (strips, strips, strips, P("dp", "tensor", None, None), P("dp", "tensor", None, None), P(), P("tensor", None))
    return jax.shard_map(body, mesh=mesh, in_specs=placed, out_specs=(strips,) * 3, check_vma=False)
```

```python
import jax
import jax.numpy as jnp
from jax import lax
from jax.experimental import pallas as pl
from jax.experimental.pallas import tpu as pltpu
from jax.sharding import PartitionSpec as P

MESH = pl.DeviceIdType.MESH
beta_first = 0.9
beta_second = 0.95
correct_first = 1.0 - 0.9**10
correct_second = 1.0 - 0.95**10
epsilon = 1e-08

ORDER = "PQssgAggBgBPggsAQPmQBPABsPBQAssPAmgBmPmQ" + "AsmmQBABmQGAhhShMhwuuuu"


def flip4(x, a):
    if a == 0:
        return x
    if a == 1:
        return x + 1 - 2 * (x % 2)
    if a == 2:
        return (x + 2) % 4
    return 3 - x


def kernel(
    grad, first, second, lcand, rcand, lown, rown,
    grot_out, upd_out,
    g_strip, f_strip, s_strip, m_send, s_send,
    g_in, m_in, s_in,
    l_half, l_quar, l_all, r_slot, r_half, r_part, r_cols, r_all,
    l_core0, l_core1, l_y0, l_y1, l_x0, l_x1, l_z0, l_z1, r_one0, r_one1, r_pair0, r_pair1, r_ring0, r_ring1,
    t_g, t_m, gsq, stp, g_send, u_send,
    send_sem, recv_sem, load_sem,
):
    dp, tn = lax.axis_index("dp"), lax.axis_index("tensor")
    ylo, z, x = dp // 32, (dp // 4) % 8, dp % 4
    yhi, core = tn // 2, tn % 2
    zlo = z % 2
    l_core, l_y, l_x, l_z = (l_core0, l_core1), (l_y0, l_y1), (l_x0, l_x1), (l_z0, l_z1)
    r_one, r_pair, r_ring = (r_one0, r_one1), (r_pair0, r_pair1), (r_ring0, r_ring1)
    p = zlo * 4 + x
    group = dp // 8

    def dev(ylo_=None, z_=None, x_=None, yhi_=None, core_=None):
        a = ylo if ylo_ is None else ylo_
        b = z if z_ is None else z_
        c = x if x_ is None else x_
        d = yhi if yhi_ is None else yhi_
        e = core if core_ is None else core_
        return (a * 32 + b * 4 + c, d * 2 + e)

    zpair = z + 1 - 2 * zlo

    def in_group(r):
        return dev(x_=flip4(x, r % 4), z_=zpair if r >= 4 else z)

    def group_place(r):
        return (1 - zlo if r >= 4 else zlo) * 4 + flip4(x, r % 4)

    def in_plane(r):
        return dev(x_=flip4(x, r % 4), ylo_=1 - ylo if r >= 4 else ylo)

    def plane_place(r):
        return (1 - ylo if r >= 4 else ylo) * 4 + flip4(x, r % 4)

    count = [0]

    def remote(src, dst, to):
        i = count[0]
        count[0] += 1
        c = pltpu.make_async_remote_copy(
            src_ref=src, dst_ref=dst, send_sem=send_sem.at[i], recv_sem=recv_sem.at[i],
            device_id=to, device_id_type=MESH,
        )
        c.start()
        return c

    lcount = [0]

    def local(src, dst):
        c = pltpu.make_async_copy(src, dst, load_sem.at[lcount[0]])
        lcount[0] += 1
        c.start()
        return c

    sent = []

    def arrive(copies):
        for c in copies:
            c.wait_recv()
        sent.extend(copies)

    ld_r = [
        local(
            rcand.at[0, 0, pl.ds(pl.multiple_of((x % 2) * 256 + h * 128, 128), 128),
                     pl.ds(pl.multiple_of((ylo * 2 + x // 2) * 128, 128), 128)],
            r_one[h].at[ylo * 4 + x],
        )
        for h in range(2)
    ]
    ld_l = [
        [
            local(
                lcand.at[0, 0, pl.ds(h * 512, 512), pl.ds(pl.multiple_of((core * 4 + j) * 128, 128), 128)],
                l_core[h].at[core, j],
            )
            for j in range(4)
        ]
        for h in range(2)
    ]
    ld_g0 = local(grad.at[pl.ds(pl.multiple_of(p * 512, 512), 512)], g_in.at[p])
    ld_g, ld_f, ld_s = local(grad, g_strip), local(first, f_strip), local(second, s_strip)

    peers = [in_group(r) for r in range(1, 8)]
    peers += [in_plane(r) for r in range(4, 8)]
    peers += [dev(z_=(z + r) % 8) for r in range(2, 7)]
    peers += [dev(z_=(z + 7 + 2 * zlo) % 8)]
    peers += [dev(yhi_=1 - yhi), dev(core_=1 - core)]
    barrier = pltpu.get_barrier_semaphore()
    for to in peers:
        pl.semaphore_signal(barrier, inc=1, device_id=to, device_id_type=MESH)
    pl.semaphore_wait(barrier, len(peers))

    lo = lown[group]
    o_core, o_yhi, o_x, o_zlo = lo % 2, (lo // 2) % 2, (lo // 4) % 4, lo // 16

    def right(slot):
        d = rown[0, (slot % 2) * 4 + slot // 2]
        return d // 32, (d // 4) % 8, d % 4

    def spread(src, dst, wait):
        for r in (4, 1, 3, 2, 5, 7, 6):
            q = group_place(r)
            wait.append(remote(src.at[pl.ds(pl.multiple_of(q * 512, 512), 512)], dst.at[p], in_group(r)))
            yield

    def left_chain(h):
        rows = pl.ds(h * 512, 512)
        wait = [
            remote(
                lcand.at[0, 0, rows, pl.ds(pl.multiple_of(((1 - core) * 4 + j) * 128, 128), 128)],
                l_core[h].at[core, j], dev(core_=1 - core),
            )
            for j in range(4)
        ]
        yield
        for c in ld_l[h]:
            c.wait()
        arrive(wait)
        l_half[h] = l_core[h][o_core]
        wait = [remote(l_half.at[h, pl.ds((1 - yhi) * 2, 2)], l_y[h].at[yhi], dev(yhi_=1 - yhi))]
        l_y[h][yhi] = l_half[h, pl.ds(yhi * 2, 2)]
        yield
        arrive(wait)
        for i in range(4):
            l_quar[h, i] = l_y[h][o_yhi, i // 2, (i % 2) * 256:(i % 2) * 256 + 256]
        wait = [remote(l_quar.at[h, flip4(x, r)], l_x[h].at[x], dev(x_=flip4(x, r))) for r in range(1, 4)]
        l_x[h][x] = l_quar[h, x]
        yield
        arrive(wait)
        l_z[h][zlo] = l_x[h][o_x]
        wait = [remote(l_z[h].at[zlo], l_z[h].at[zlo], dev(z_=zpair))]
        yield
        arrive(wait)
        mine = l_all.at[core * 4 + yhi * 2 + x // 2, h, x % 2]
        mine[...] = l_z[h][o_zlo]
        wait = [remote(mine, mine, dev(x_=flip4(x, r))) for r in range(1, 4)]
        yield
        arrive(wait)
        mine = l_all.at[pl.ds(core * 4 + yhi * 2, 2), h]
        wait = [remote(mine, mine, dev(yhi_=1 - yhi))]
        yield
        arrive(wait)
        mine = l_all.at[pl.ds(core * 4, 4), h]
        wait = [remote(mine, mine, dev(core_=1 - core))]
        yield
        arrive(wait)
        yield

    def right_chain(h):
        wait = []
        for r in range(1, 8):
            q = plane_place(r)
            wait.append(remote(
                rcand.at[0, 0, pl.ds(pl.multiple_of((q % 2) * 256 + h * 128, 128), 128),
                         pl.ds(pl.multiple_of((q // 2) * 128, 128), 128)],
                r_one[h].at[ylo * 4 + x], in_plane(r),
            ))
        yield
        ld_r[h].wait()
        arrive(wait)
        for s in range(8):
            oy, oz, ox = right(s)
            r_slot[h, s] = r_one[h][oy * 4 + ox]
        wait = [remote(
            r_slot.at[h, :, pl.ds(pl.multiple_of((1 - zlo) * 64, 64), 64)], r_pair[h].at[zlo],
            dev(z_=(z + 7 + 2 * zlo) % 8),
        )]
        r_pair[h][zlo] = r_slot[h, :, pl.ds(pl.multiple_of(zlo * 64, 64), 64)]
        yield
        arrive(wait)
        for s in range(8):
            oy, oz, ox = right(s)
            r_half[h, s] = r_pair[h][oz % 2, s]
        ring = ((z + 1) // 2) % 4
        wait = [
            remote(
                r_half.at[h, :, pl.ds(pl.multiple_of(((ring + r) % 4) * 16, 16), 16)], r_ring[h].at[ring],
                dev(z_=(z + 2 * r) % 8),
            )
            for r in range(1, 4)
        ]
        r_ring[h][ring] = r_half[h, :, pl.ds(pl.multiple_of(ring * 16, 16), 16)]
        yield
        arrive(wait)
        for s in range(8):
            oy, oz, ox = right(s)
            r_part[h, s // 2, s % 2] = r_ring[h][((oz + 1) // 2) % 4, s]
        wait = [remote(r_part.at[h, flip4(x, r)], r_cols.at[h, x], dev(x_=flip4(x, r))) for r in range(1, 4)]
        r_cols[h, x] = r_part[h, x]
        yield
        arrive(wait)
        sub = zlo * 4 + ring
        wait = [
            remote(
                r_cols.at[h, :, (z + r) % 2], r_all.at[pl.ds(ylo * 4, 4), h, sub], dev(z_=(z + r) % 8),
            )
            for r in range(1, 8)
        ]
        r_all[pl.ds(ylo * 4, 4), h, sub] = r_cols[h, :, zlo]
        yield
        arrive(wait)
        mine = r_all.at[pl.ds(ylo * 4, 4), h]
        wait = [remote(mine, mine, dev(ylo_=1 - ylo))]
        yield
        arrive(wait)
        yield

    def right_basis():
        return jnp.concatenate([r_all[2 * j:2 * j + 2].reshape(512, 128) for j in range(4)], axis=1)

    def turn(src, dst):
        basis = right_basis()

        def one(j, carry):
            cols = jnp.concatenate([src[2 * j], src[2 * j + 1]], axis=1)
            t = lax.dot_general(basis, cols, (((0,), (0,)), ((), ())), preferred_element_type=jnp.float32)
            dst[:, pl.ds(pl.multiple_of(j * 256, 256), 256)] = t.astype(jnp.bfloat16)
            return carry

        lax.fori_loop(0, 4, one, 0)

    def gradient_chain():
        wait = []
        yield from spread(grad, g_in, wait)
        ld_g0.wait()
        arrive(wait)
        turn(g_in, t_g)
        yield

    def moment_chain():
        ld_g.wait()
        ld_f.wait()

        def fold(i, carry):
            rows = pl.ds(pl.multiple_of(i * 256, 256), 256)
            m_send[rows] = (
                beta_first * f_strip[rows] + (1.0 - beta_first) * g_strip[rows].astype(jnp.float32)
            ).astype(jnp.bfloat16)
            return carry

        lax.fori_loop(0, 16, fold, 0)
        m_in[p] = m_send[pl.ds(pl.multiple_of(p * 512, 512), 512)]
        wait = []
        yield from spread(m_send, m_in, wait)
        arrive(wait)
        turn(m_in, t_m)
        yield

    def second_chain():
        ld_s.wait()

        def narrow(i, carry):
            rows = pl.ds(pl.multiple_of(i * 256, 256), 256)
            s_send[rows] = s_strip[rows].astype(jnp.bfloat16)
            return carry

        lax.fori_loop(0, 16, narrow, 0)
        s_in[p] = s_send[pl.ds(pl.multiple_of(p * 512, 512), 512)]
        wait = []
        yield from spread(s_send, s_in, wait)
        arrive(wait)
        yield

    def pair_at(s):
        return (1 - zlo if s >= 2 else zlo) * 2 + (1 - x // 2 if s % 2 else x // 2)

    def left_cols(j):
        return jnp.concatenate(
            [l_all[2 * j].reshape(1024, 128), l_all[2 * j + 1].reshape(1024, 128)], axis=1
        )

    home = pl.ds(pl.multiple_of(p * 512, 512), 512)
    back, back_local = [], []

    def send_home(buf, out, s):
        for r in (2 * s, 2 * s + 1):
            q = group_place(r)
            if r == 0:
                back_local.append(local(buf.at[q], out.at[home]))
            else:
                back.append(remote(buf.at[q], out.at[home], in_group(r)))

    def home_gradient():
        for s in (2, 0, 1, 3):
            j = pair_at(s)
            g = jnp.dot(t_g[...], left_cols(j), preferred_element_type=jnp.float32)
            gsq[j] = g * g
            low = g.astype(jnp.bfloat16)
            g_send[2 * j] = low[:, :128]
            g_send[2 * j + 1] = low[:, 128:]
            send_home(g_send, grot_out, s)
            yield

    def make_step():
        def left_moment(j, carry):
            m = jnp.dot(t_m[...], left_cols(j), preferred_element_type=jnp.float32)
            old = jnp.concatenate([s_in[2 * j], s_in[2 * j + 1]], axis=1).astype(jnp.float32)
            new = beta_second * old + (1.0 - beta_second) * gsq[j]
            step = m / (correct_first * (jnp.sqrt(new * (1.0 / correct_second)) + epsilon))
            stp[:, pl.ds(pl.multiple_of(j * 256, 256), 256)] = step.astype(jnp.bfloat16)
            return carry

        lax.fori_loop(0, 4, left_moment, 0)
        yield

    def home_update():
        for s in (2, 0, 1, 3):
            j = pair_at(s)
            rows = jnp.concatenate([l_all[b, j // 2, j % 2] for b in range(8)], axis=1)
            image = lax.dot_general(
                stp[...], rows, (((1,), (1,)), ((), ())), preferred_element_type=jnp.float32
            ).astype(jnp.bfloat16)
            out = jnp.dot(right_basis(), image, preferred_element_type=jnp.float32).astype(jnp.bfloat16)
            u_send[2 * j] = out[:, :128]
            u_send[2 * j + 1] = out[:, 128:]
            send_home(u_send, upd_out, s)
            yield

    g, m, s = gradient_chain(), moment_chain(), second_chain()
    chains = {
        "A": left_chain(0), "B": left_chain(1), "P": right_chain(0), "Q": right_chain(1),
        "g": g, "G": g, "m": m, "M": m, "s": s, "S": s,
        "h": home_gradient(), "w": make_step(), "u": home_update(),
    }
    for name in ORDER:
        next(chains[name])

    arrive(back)
    for c in back_local:
        c.wait()
    for c in sent:
        c.wait_send()


def body(gradient, first_moment, second_moment, left_candidates, right_candidates, left_owner, right_owner):
    bf, f32 = jnp.bfloat16, jnp.float32
    any_, smem = pl.BlockSpec(memory_space=pl.ANY), pl.BlockSpec(memory_space=pltpu.SMEM)
    vm = pltpu.VMEM
    strip = jax.ShapeDtypeStruct(gradient.shape, bf)
    grot, update = pl.pallas_call(
        kernel,
        name="soap_swap",
        out_shape=(strip, strip),
        in_specs=[any_] * 5 + [smem] * 2,
        out_specs=(any_, any_),
        scratch_shapes=[
            vm((4096, 128), bf), vm((4096, 128), f32), vm((4096, 128), f32), vm((4096, 128), bf), vm((4096, 128), bf),
            vm((8, 512, 128), bf), vm((8, 512, 128), bf), vm((8, 512, 128), bf),
            vm((2, 4, 512, 128), bf), vm((2, 4, 256, 128), bf), vm((8, 2, 2, 256, 128), bf),
            vm((2, 8, 128, 128), bf), vm((2, 8, 64, 128), bf), vm((2, 4, 2, 16, 128), bf), vm((2, 4, 2, 16, 128), bf),
            vm((8, 2, 8, 16, 128), bf),
            *[vm((2, 4, 512, 128), bf)] * 2, *[vm((2, 2, 512, 128), bf)] * 2,
            *[vm((4, 256, 128), bf)] * 2, *[vm((2, 256, 128), bf)] * 2,
            *[vm((8, 128, 128), bf)] * 2, *[vm((2, 8, 64, 128), bf)] * 2, *[vm((4, 8, 16, 128), bf)] * 2,
            vm((512, 1024), bf), vm((512, 1024), bf), vm((4, 512, 256), f32), vm((512, 1024), bf),
            vm((8, 512, 128), bf), vm((8, 512, 128), bf),
            pltpu.SemaphoreType.DMA((112,)), pltpu.SemaphoreType.DMA((112,)), pltpu.SemaphoreType.DMA((24,)),
        ],
        compiler_params=pltpu.CompilerParams(
            collective_id=0, has_side_effects=True, vmem_limit_bytes=56 * 2**20
        ),
    )(gradient, first_moment, second_moment, left_candidates, right_candidates, left_owner, right_owner)
    moment_new = beta_first * first_moment + (1.0 - beta_first) * gradient.astype(f32)
    turned = grot.astype(f32)
    second_new = beta_second * second_moment + (1.0 - beta_second) * turned * turned
    return moment_new, second_new, update


def solution(mesh):
    strips = P("tensor", "dp")
    placed = (strips, strips, strips, P("dp", "tensor", None, None), P("dp", "tensor", None, None), P(), P("tensor", None))
    return jax.shard_map(body, mesh=mesh, in_specs=placed, out_specs=(strips,) * 3, check_vma=False)
```
